512 devices in a mesh: patch: 16 (over z, core), epoch: 8 (over y_hi, x), band: 4 (over y_lo).
Axes of the slice: x: 4, y: 8 (y_hi: 2, y_lo: 4; y = y_hi * 4 + y_lo), z: 8, core: 2. Of those that a mesh axis runs over, the one named last changes fastest.
Arguments:
- exposures: bfloat16 [64, 2048, 2048], P(('band', 'epoch'), 'patch'), parts along dimension 0, may hold values from -6 to 6
- inv_variance: bfloat16 [64, 2048, 2048], P(('band', 'epoch'), 'patch'), parts along dimension 0, may hold values from 0.25 to 4
- strip_bounds: int32 [64, 2], P(('band', 'epoch')), parts along dimension 0, may hold values from 0 to 16, as said below
- kernel_index: int32 [64, 2, 2], P(('band', 'epoch')), parts along dimension 0, may hold values from 0 to 15
- basis_bank: float32 [16, 21], replicated, may hold values from 0.05 to 1
Outputs:
- coadd: float32 [8192, 2048], P(('band', 'patch'), 'epoch'), parts along dimension 0
- depth_map: float32 [8192, 2048], P(('band', 'patch'), 'epoch'), parts along dimension 0
The draws below stay inside these ranges and needn't reach their ends.
There are 4 independent parts, one for each index of `band`. The reference program is written for one: setup_inputs(seed, part) draws one part's arguments, and reference() takes and returns one part's arrays. A program takes and returns all parts, laid end to end along the dimension named above; an argument that names none is the same for every part. Nothing has to cross between parts.
Inputs may be any that keep to these rules, and one draw needn't show every extreme that they name: `strip_bounds`: each row is a pair lower < upper of strip units; exposure 0 covers the whole window.
All inputs are finite; a program needn't handle non-finite values.
Results may differ from the reference program's by a relative error of at most 0.0043.
Values may be sent and summed in bfloat16 or wider, within the bound.
No kernel may reach another device: no remote copies, remote signals or barrier semaphores. Data moves between devices by JAX's collectives and lax.ppermute only.
A program may use at most 64 MiB of HBM per device.

```python
import math
import jax
import jax.numpy as jnp
from jax import lax

WIDTH = 2048
UNIT = 128
HALF = 10
TAPS = 21
NBASIS = 16
NCOMP = 2
EXPOSURES = 16
ROWS_ALL = 2048
UNITS = 16


def draw_strip_bounds(key, part):
    key = jax.random.fold_in(key, 11)
    key = jax.random.fold_in(key, part)
    start_key, extent_key = jax.random.split(key)
    lower_unit = jax.random.randint(start_key, (EXPOSURES,), 0, UNITS)
    extent = jax.random.randint(extent_key, (EXPOSURES,), 1, UNITS + 1)
    upper_unit = jnp.minimum(lower_unit + extent, UNITS)
    leading = jnp.arange(EXPOSURES) == 0
    lower_unit = jnp.where(leading, 0, lower_unit)
    upper_unit = jnp.where(leading, UNITS, upper_unit)
    return jnp.stack([lower_unit, upper_unit], axis=1).astype(jnp.int32)


def set_ends(entries, stream_key, smallest, largest):
    place = [jax.random.randint(jax.random.fold_in(stream_key, axis), (), 0, length) for axis, length in enumerate(entries.shape)]
    longest = entries.shape.index(max(entries.shape))
    neighbour = place[:longest] + [(place[longest] + 1) % entries.shape[longest]] + place[longest + 1:]
    return entries.at[tuple(place)].set(smallest).at[tuple(neighbour)].set(largest)


def levels(rng, dims, shards, low, top_value):
    loudness, own = 1.0, jax.random.fold_in(rng, 6)
    for axis_at, blocks in shards:
        heights = jnp.exp(jax.random.uniform(jax.random.fold_in(own, axis_at), (blocks,), jnp.float32, low / len(shards), top_value / len(shards)))
        loudness = loudness * jnp.repeat(heights, dims[axis_at] // blocks).reshape([-1 if axis == axis_at else 1 for axis in range(len(dims))])
    return loudness


def bell_draw(stream_key, shape, scale, limit, cuts=(), kind=jnp.bfloat16):
    entries = scale * jax.random.normal(stream_key, shape, jnp.float32)
    if cuts:
        entries = entries * levels(stream_key, shape, cuts, -0.22, 0.18)
    return jnp.clip(entries, -limit, limit).astype(kind)


def setup_inputs(seed: int = 0, part: int = 0) -> dict:
    splits = jax.random.split(jax.random.key(seed), 6)
    own_keys = jax.random.split(jax.random.fold_in(splits[5], part), 6)
    return {
        "exposures": bell_draw(own_keys[0], (EXPOSURES, ROWS_ALL, WIDTH), 1.0, 6.0, ((0, 8), (1, 16))),
        "inv_variance": jnp.clip(jnp.exp(math.log(4.0) - 2.7725887 * jax.random.uniform(own_keys[1], (EXPOSURES, ROWS_ALL, WIDTH), jnp.float32) ** levels(own_keys[1], (EXPOSURES, ROWS_ALL, WIDTH), ((0, 8), (1, 16)), -0.2, 0.2)), 0.25, 4.0).astype(jnp.bfloat16),
        "strip_bounds": draw_strip_bounds(jax.random.fold_in(jax.random.fold_in(splits[5], part), 71), part),
        "kernel_index": set_ends(jax.random.randint(own_keys[3], (EXPOSURES, NCOMP, 2), 0, NBASIS), jax.random.fold_in(own_keys[3], 1), 0, NBASIS - 1).astype(jnp.int32),
        "basis_bank": jnp.clip(jnp.exp(jax.random.uniform(splits[4], (NBASIS, TAPS), jnp.float32, math.log(0.05), math.log(1.0))), 0.05, 1.0),
    }


def select_taps(basis_bank, which, factor):
    chosen = basis_bank[which]
    return ((chosen / jnp.sum(chosen)) * factor).astype(jnp.bfloat16).astype(jnp.float32)


def reference(exposures, inv_variance, strip_bounds, kernel_index, basis_bank):
    row_ids = jnp.arange(ROWS_ALL, dtype=jnp.int32)
    numer = jnp.zeros((ROWS_ALL, WIDTH), jnp.float32)
    denom = jnp.zeros((ROWS_ALL, WIDTH), jnp.float32)
    for index in range(EXPOSURES):
        covered = (row_ids >= strip_bounds[index, 0] * UNIT) & (row_ids < strip_bounds[index, 1] * UNIT)
        pixels = jnp.where(covered[:, None], exposures[index].astype(jnp.float32), 0.0)
        weights = jnp.where(covered[:, None], inv_variance[index].astype(jnp.float32), 0.0)
        smoothed = jnp.zeros((ROWS_ALL, WIDTH), jnp.float32)
        for comp in range(NCOMP):
            row_taps = select_taps(basis_bank, kernel_index[index, comp, 0], 1.0)
            column_taps = select_taps(basis_bank, kernel_index[index, comp, 1], 1.0 / NCOMP)
            padded = jnp.pad(pixels, ((0, 0), (HALF, HALF)))
            across = jnp.zeros((ROWS_ALL, WIDTH), jnp.float32)
            for offset in range(TAPS):
                across = across + row_taps[offset] * padded[:, offset:offset + WIDTH]
            across = lax.optimization_barrier(across.astype(jnp.bfloat16)).astype(jnp.float32)
            padded = jnp.pad(across, ((HALF, HALF), (0, 0)))
            for offset in range(TAPS):
                smoothed = smoothed + column_taps[offset] * padded[offset:offset + ROWS_ALL]
        numer = numer + weights * smoothed
        denom = denom + weights
    return numer / jnp.maximum(denom, 1.0), denom
```

```python
import functools

import jax
import jax.numpy as jnp
from jax import lax
from jax.experimental import pallas as pl
from jax.experimental.pallas import tpu as pltpu
from jax.sharding import PartitionSpec as P

UNIT = 128
HALF = 10
TAPS = 21
NCOMP = 2
LANES = 128
EDGE = 16
TRANSPOSED = (((1,), (1,)), ((), ()))


def toeplitz(base, rows, shift):
    width = base.shape[1]
    wide = jnp.broadcast_to(base, (rows, width))
    if shift:
        wide = pltpu.roll(wide, shift % width, 1)
    return pltpu.roll(wide, 0, 1, stride=1, stride_axis=0)


def matrices(index_ref, bank_ref, row_ref, own_ref, edge_ref):
    exp_count = row_ref.shape[0]
    lane = lax.broadcasted_iota(jnp.int32, (EDGE, LANES), 1)
    for exp in range(exp_count):
        edge_top = jnp.zeros((EDGE, LANES), jnp.float32)
        edge_bottom = jnp.zeros((EDGE, LANES), jnp.float32)
        for comp in range(NCOMP):
            bases = []
            for side in range(2):
                taps = bank_ref[pl.ds(index_ref[exp, 2 * comp + side], 1), :]
                taps = taps / jnp.sum(taps, axis=1, keepdims=True)
                if side == 1:
                    taps = taps * (1.0 / NCOMP)
                taps = taps.astype(jnp.bfloat16).astype(jnp.float32)
                bases.append(
                    jnp.concatenate([taps, jnp.zeros((1, 2 * LANES - TAPS), jnp.float32)], axis=1)
                )
            row_ref[exp, comp * LANES : (comp + 1) * LANES, :] = toeplitz(bases[0], LANES, 0).astype(jnp.bfloat16)
            wide = toeplitz(bases[1], UNIT, -HALF)
            own_ref[exp, :, comp * UNIT : (comp + 1) * UNIT] = wide[:, :UNIT].astype(jnp.bfloat16)
            short = bases[1][:, :LANES]
            first = comp * EDGE
            top = toeplitz(short, EDGE, first + EDGE - HALF)
            edge_top = jnp.where((lane >= first) & (lane < first + EDGE), top, edge_top)
            first = (NCOMP + comp) * EDGE
            bottom = toeplitz(short, EDGE, first - EDGE - HALF)
            edge_bottom = jnp.where((lane >= first) & (lane < first + EDGE), bottom, edge_bottom)
        edge_ref[exp, :EDGE, :] = edge_top.astype(jnp.bfloat16)
        edge_ref[exp, EDGE:, :] = edge_bottom.astype(jnp.bfloat16)


def partial_sums(
    bounds_ref, place_ref, pixels_ref, above_ref, below_ref, variance_ref, row_ref, own_ref, edge_ref,
    out_ref, window_ref, across_ref, halo_ref, numer_ref, denom_ref,
):
    exp = pl.program_id(0)
    last = pl.num_programs(0) - 1
    unit = place_ref[0]
    lower, upper = bounds_ref[exp, 0], bounds_ref[exp, 1]

    def covers(at):
        return jnp.where((at >= lower) & (at < upper), 1.0, 0.0)

    width = pixels_ref.shape[2]
    blocks = width // LANES
    rows = UNIT + 2 * EDGE
    pixels = jnp.concatenate(
        [
            pixels_ref[0].astype(jnp.float32),
            above_ref[0].astype(jnp.float32) * covers(unit - 1),
            below_ref[0].astype(jnp.float32) * covers(unit + 1),
        ],
        axis=0,
    )
    moved = pltpu.roll(pixels, HALF, 1)
    lane = lax.broadcasted_iota(jnp.int32, (rows, LANES), 1)
    head = moved[:, :LANES]
    window_ref[:, :LANES] = jnp.where(lane < HALF, 0.0, head).astype(jnp.bfloat16)
    window_ref[:, LANES:width] = moved[:, LANES:].astype(jnp.bfloat16)
    window_ref[:, width:] = jnp.where(lane < HALF, head, 0.0).astype(jnp.bfloat16)
    for block in range(blocks):
        at = slice(block * LANES, (block + 1) * LANES)
        filtered = lax.dot_general(
            window_ref[:, block * LANES : (block + 2) * LANES],
            row_ref[0],
            TRANSPOSED,
            preferred_element_type=jnp.float32,
        ).astype(jnp.bfloat16)
        for comp in range(NCOMP):
            mine = filtered[:, comp * LANES : (comp + 1) * LANES]
            across_ref[comp * UNIT : (comp + 1) * UNIT, at] = mine[:UNIT]
            halo_ref[comp * EDGE : (comp + 1) * EDGE, at] = mine[UNIT : UNIT + EDGE]
            first = (NCOMP + comp) * EDGE
            halo_ref[first : first + EDGE, at] = mine[UNIT + EDGE :]
    weights = variance_ref[0].astype(jnp.float32) * covers(unit)
    smoothed = jnp.dot(own_ref[0], across_ref[...], preferred_element_type=jnp.float32)
    edges = jnp.dot(
        edge_ref[0, :, : 2 * NCOMP * EDGE], halo_ref[...], preferred_element_type=jnp.float32
    )
    smoothed = jnp.concatenate(
        [smoothed[:EDGE] + edges[:EDGE], smoothed[EDGE : UNIT - EDGE], smoothed[UNIT - EDGE :] + edges[EDGE:]],
        axis=0,
    )
    term = weights * smoothed

    @pl.when(exp == 0)
    def _():
        numer_ref[...] = term
        denom_ref[...] = weights

    @pl.when(exp > 0)
    def _():
        numer_ref[...] += term
        denom_ref[...] += weights

    @pl.when(exp == last)
    def _():
        parts, _, share = out_ref.shape
        for part in range(parts):
            at = slice(part * share, (part + 1) * share)
            out_ref[part, :UNIT, :] = numer_ref[:, at].astype(jnp.bfloat16)
            out_ref[part, UNIT:, :] = denom_ref[:, at].astype(jnp.bfloat16)


def finish(parts_ref, coadd_ref, depth_ref):
    numer = jnp.sum(parts_ref[:, :UNIT, :].astype(jnp.float32), axis=0)
    denom = jnp.sum(parts_ref[:, UNIT:, :].astype(jnp.float32), axis=0)
    coadd_ref[...] = numer / jnp.maximum(denom, 1.0)
    depth_ref[...] = denom


def whole(shape):
    return pl.BlockSpec(shape, lambda *_: (0,) * len(shape))


def each(shape):
    return pl.BlockSpec((1,) + shape[1:], lambda exp: (exp,) + (0,) * (len(shape) - 1))


def shards(exposures, inv_variance, strip_bounds, kernel_index, basis_bank):
    exp_count, row_count, width = exposures.shape
    patches, parts = lax.axis_size("patch"), lax.axis_size("epoch")
    share = width // parts
    down = [(i, i + 1) for i in range(patches - 1)]
    up = [(i + 1, i) for i in range(patches - 1)]
    above = lax.ppermute(exposures[:, row_count - EDGE :], "patch", down)
    below = lax.ppermute(exposures[:, :EDGE], "patch", up)
    smem = pl.BlockSpec(memory_space=pltpu.SMEM)
    row_mats, own_mats, edge_mats = pl.pallas_call(
        matrices,
        out_shape=(
            jax.ShapeDtypeStruct((exp_count, NCOMP * LANES, 2 * LANES), jnp.bfloat16),
            jax.ShapeDtypeStruct((exp_count, UNIT, NCOMP * UNIT), jnp.bfloat16),
            jax.ShapeDtypeStruct((exp_count, 2 * EDGE, LANES), jnp.bfloat16),
        ),
        in_specs=[smem, whole(basis_bank.shape)],
        name="band_matrices",
    )(kernel_index.reshape(exp_count, 2 * NCOMP), basis_bank)
    place = lax.axis_index("patch").reshape(1).astype(jnp.int32)
    sums = pl.pallas_call(
        partial_sums,
        out_shape=jax.ShapeDtypeStruct((parts, 2 * row_count, share), jnp.bfloat16),
        grid=(exp_count,),
        in_specs=[
            smem,
            smem,
            each(exposures.shape),
            each(above.shape),
            each(below.shape),
            each(inv_variance.shape),
            each(row_mats.shape),
            each(own_mats.shape),
            each(edge_mats.shape),
        ],
        out_specs=whole((parts, 2 * row_count, share)),
        scratch_shapes=[
            pltpu.VMEM((UNIT + 2 * EDGE, width + LANES), jnp.bfloat16),
            pltpu.VMEM((NCOMP * UNIT, width), jnp.bfloat16),
            pltpu.VMEM((2 * NCOMP * EDGE, width), jnp.bfloat16),
            pltpu.VMEM((row_count, width), jnp.float32),
            pltpu.VMEM((row_count, width), jnp.float32),
        ],
        compiler_params=pltpu.CompilerParams(vmem_limit_bytes=32 * 1024 * 1024),
        name="partial_sums",
    )(strip_bounds, place, exposures, above, below, inv_variance, row_mats, own_mats, edge_mats)
    received = lax.all_to_all(sums, "epoch", 0, 0, tiled=True)
    out = jax.ShapeDtypeStruct((row_count, share), jnp.float32)
    return pl.pallas_call(finish, out_shape=(out, out), name="finish")(received)


def solution(mesh):
    return jax.shard_map(
        shards,
        mesh=mesh,
        in_specs=(
            P(("band", "epoch"), "patch", None),
            P(("band", "epoch"), "patch", None),
            P(("band", "epoch"), None),
            P(("band", "epoch"), None, None),
            P(),
        ),
        out_specs=(P(("band", "patch"), "epoch"), P(("band", "patch"), "epoch")),
        check_vma=False,
    )
```

```python
import jax
import jax.numpy as jnp
from jax import lax
from jax.experimental import pallas as pl
from jax.experimental.pallas import tpu as pltpu
from jax.sharding import PartitionSpec as P

UNIT = 128
HALF = 10
TAPS = 21
NCOMP = 2
LANES = 128
EDGE = 16
FAR = 2
GROUP = 4
CHUNK = 32
TRANSPOSED = (((1,), (1,)), ((), ()))


def toeplitz(base, rows, shift):
    width = base.shape[1]
    if shift:
        base = pltpu.roll(base, shift % width, 1)
    return pltpu.roll(jnp.broadcast_to(base, (rows, width)), 0, 1, stride=1, stride_axis=0)


def matrices(index_ref, exp, taps_ref, row_ref, own_ref, edge_ref):
    lane = lax.broadcasted_iota(jnp.int32, (EDGE, LANES), 1)
    edge_top = jnp.zeros((EDGE, LANES), jnp.float32)
    edge_bottom = jnp.zeros((EDGE, LANES), jnp.float32)
    for comp in range(NCOMP):
        base = taps_ref[pl.ds(index_ref[exp, comp, 0], 1), :]
        row_ref[exp, comp * LANES : (comp + 1) * LANES, :] = toeplitz(base, LANES, 0).astype(jnp.bfloat16)
        base = taps_ref[pl.ds(index_ref[exp, comp, 1], 1), :] * (1.0 / NCOMP)
        wide = toeplitz(base, UNIT, -HALF)
        own_ref[exp, :, comp * UNIT : (comp + 1) * UNIT] = wide[:, :UNIT].astype(jnp.bfloat16)
        short = base[:, :LANES]
        first = comp * EDGE
        top = toeplitz(short, EDGE, first + EDGE - HALF)
        edge_top = jnp.where((lane >= first) & (lane < first + EDGE), top, edge_top)
        first = (NCOMP + comp) * EDGE
        bottom = toeplitz(short, EDGE, first - EDGE - HALF)
        edge_bottom = jnp.where((lane >= first) & (lane < first + EDGE), bottom, edge_bottom)
    edge_ref[exp, :EDGE, :] = edge_top.astype(jnp.bfloat16)
    edge_ref[exp, EDGE:, :] = edge_bottom.astype(jnp.bfloat16)


def mask(bounds_ref, exp, unit):
    return jnp.where((unit >= bounds_ref[exp, 0]) & (unit < bounds_ref[exp, 1]), 1.0, 0.0)


def fill_window(window_ref, exp, pixels):
    rows, width = pixels.shape
    moved = pltpu.roll(pixels, HALF, 1)
    lane = lax.broadcasted_iota(jnp.int32, (rows, LANES), 1)
    head = moved[:, :LANES]
    window_ref[exp, :, :LANES] = jnp.where(lane < HALF, 0.0, head).astype(jnp.bfloat16)
    window_ref[exp, :, LANES:width] = moved[:, LANES:].astype(jnp.bfloat16)
    window_ref[exp, :, width:] = jnp.where(lane < HALF, head, 0.0).astype(jnp.bfloat16)


def row_filter(window_ref, exp, matrix, start, count):
    stacked = jnp.concatenate(
        [window_ref[exp, :, block * LANES : (block + 2) * LANES] for block in range(start, start + count)], axis=0
    )
    return lax.dot_general(stacked, matrix, TRANSPOSED, preferred_element_type=jnp.float32).astype(jnp.bfloat16)


def spread(out_ref, value, rows=slice(None)):
    near, _, _, share = out_ref.shape
    for part in range(value.shape[1] // share):
        y, x = divmod(part, near)
        out_ref[x, y, rows, :] = value[:, part * share : (part + 1) * share].astype(out_ref.dtype)


def weight_sums(
    bounds_hbm, pixels_hbm, variance_hbm, denom_hbm, first_hbm, last_hbm,
    bounds_ref, first_ref, last_ref, variance_ref, denom_ref, in_sems, out_sems, side_sems,
):
    unit = lax.axis_index("patch")
    exp_count, rows, _ = variance_ref.shape
    chunks = [pl.ds(at, CHUNK) for at in range(0, rows, CHUNK)]
    sides = [
        pltpu.make_async_copy(bounds_hbm, bounds_ref, side_sems.at[0]),
        pltpu.make_async_copy(pixels_hbm.at[:, pl.ds(0, EDGE)], first_ref, side_sems.at[1]),
        pltpu.make_async_copy(pixels_hbm.at[:, pl.ds(rows - EDGE, EDGE)], last_ref, side_sems.at[2]),
    ]
    strips = [
        pltpu.make_async_copy(first_ref, first_hbm, side_sems.at[3]),
        pltpu.make_async_copy(last_ref, last_hbm, side_sems.at[4]),
    ]
    arrivals = [
        pltpu.make_async_copy(variance_hbm.at[:, at], variance_ref.at[:, at], in_sems.at[i])
        for i, at in enumerate(chunks)
    ]
    leaves = [
        pltpu.make_async_copy(denom_ref.at[:, :, at], denom_hbm.at[:, :, at], out_sems.at[i])
        for i, at in enumerate(chunks)
    ]
    for copy in sides + arrivals:
        copy.start()
    for copy in sides:
        copy.wait()
    for copy in strips:
        copy.start()
    masks = [mask(bounds_ref, exp, unit) for exp in range(exp_count)]
    for i, at in enumerate(chunks):
        arrivals[i].wait()
        denom = variance_ref[0, at, :].astype(jnp.float32) * masks[0]
        for exp in range(1, exp_count):
            denom += variance_ref[exp, at, :].astype(jnp.float32) * masks[exp]
        spread(denom_ref, denom, at)
        leaves[i].start()
    for copy in leaves + strips:
        copy.wait()


def weighted_sums(
    index_hbm, bounds_hbm, bank_hbm, above_hbm, below_hbm, pixels_hbm, variance_hbm, out_hbm,
    index_ref, bounds_ref, bank_ref, above_ref, below_ref,
    out_ref, taps_ref, row_ref, own_ref, edge_ref, pixels_ref, variance_ref, window_ref, across_ref, halo_ref,
    sems, side_sems, out_sems,
):
    unit = lax.axis_index("patch")
    exp_count, rows, width = pixels_ref.shape
    sides = [
        pltpu.make_async_copy(source, target, side_sems.at[i])
        for i, (source, target) in enumerate(
            (
                (index_hbm, index_ref),
                (bank_hbm, bank_ref),
                (bounds_hbm, bounds_ref),
                (above_hbm, above_ref),
                (below_hbm, below_ref),
            )
        )
    ]
    pixel_copies = [pltpu.make_async_copy(pixels_hbm.at[e], pixels_ref.at[e], sems.at[e]) for e in range(exp_count)]
    weight_copies = [
        pltpu.make_async_copy(variance_hbm.at[e], variance_ref.at[e], sems.at[exp_count + e]) for e in range(exp_count)
    ]
    for copy in sides:
        copy.start()
    for pair in zip(pixel_copies, weight_copies):
        for copy in pair:
            copy.start()
    for copy in sides:
        copy.wait()
    bank = bank_ref[...]
    bank = (bank / jnp.sum(bank, axis=1, keepdims=True)).astype(jnp.bfloat16).astype(jnp.float32)
    taps_ref[...] = jnp.concatenate([bank, jnp.zeros((bank.shape[0], 2 * LANES - TAPS), jnp.float32)], axis=1)
    for exp in range(exp_count):
        matrices(index_ref, exp, taps_ref, row_ref, own_ref, edge_ref)
    total = rows + 2 * EDGE
    for exp in range(exp_count):
        pixel_copies[exp].wait()
        above = above_ref[exp].astype(jnp.float32) * mask(bounds_ref, exp, unit - 1)
        below = below_ref[exp].astype(jnp.float32) * mask(bounds_ref, exp, unit + 1)
        fill_window(window_ref, exp, jnp.concatenate([pixels_ref[exp].astype(jnp.float32), above, below], axis=0))
        for start in range(0, width // LANES, GROUP):
            filtered = row_filter(window_ref, exp, row_ref[exp], start, GROUP)
            for block in range(GROUP):
                at = slice((start + block) * LANES, (start + block + 1) * LANES)
                for comp in range(NCOMP):
                    mine = filtered[block * total : (block + 1) * total, comp * LANES : (comp + 1) * LANES]
                    across_ref[exp, comp * UNIT : (comp + 1) * UNIT, at] = mine[:UNIT]
                    halo_ref[exp, comp * EDGE : (comp + 1) * EDGE, at] = mine[UNIT : UNIT + EDGE]
                    first = (NCOMP + comp) * EDGE
                    halo_ref[exp, first : first + EDGE, at] = mine[UNIT + EDGE :]
    for copy in weight_copies:
        copy.wait()
    masks = [mask(bounds_ref, exp, unit) for exp in range(exp_count)]
    near, _, _, share = out_ref.shape
    leaves = []
    for part in range(width // share):
        y, x = divmod(part, near)
        at = slice(part * share, (part + 1) * share)
        numer = jnp.zeros((rows, share), jnp.float32)
        for exp in range(exp_count):
            smoothed = jnp.dot(own_ref[exp], across_ref[exp, :, at], preferred_element_type=jnp.float32)
            edges = jnp.dot(
                edge_ref[exp, :, : 2 * NCOMP * EDGE], halo_ref[exp, :, at], preferred_element_type=jnp.float32
            )
            smoothed = jnp.concatenate(
                [smoothed[:EDGE] + edges[:EDGE], smoothed[EDGE : UNIT - EDGE], smoothed[UNIT - EDGE :] + edges[EDGE:]],
                axis=0,
            )
            numer += variance_ref[exp, :, at].astype(jnp.float32) * masks[exp] * smoothed
        out_ref[x, y] = numer.astype(out_ref.dtype)
        leaves.append(pltpu.make_async_copy(out_ref.at[x, y], out_hbm.at[x, y], out_sems.at[part]))
        leaves[-1].start()
    for copy in leaves:
        copy.wait()


def shards(exposures, inv_variance, strip_bounds, kernel_index, basis_bank):
    exp_count, row_count, width = exposures.shape
    patches, parts = lax.axis_size("patch"), lax.axis_size("epoch")
    near = parts // FAR
    share = width // parts
    f32, bf16 = jnp.float32, jnp.bfloat16
    hbm = pl.BlockSpec(memory_space=pl.ANY)
    far = lax.axis_index("epoch") // near
    groups = [[y * near + x for x in range(near)] for y in range(FAR)]
    swap = [(at, (at + near) % parts) for at in range(parts)]
    sends = jax.ShapeDtypeStruct((near, FAR, row_count, share), bf16)
    strip = jax.ShapeDtypeStruct((exp_count, EDGE, width), bf16)

    def reduce_near(sums):
        received = lax.all_to_all(sums, "epoch", 0, 0, tiled=True, axis_index_groups=groups)
        halves = jnp.sum(received.astype(f32), axis=0)
        return jnp.where(far == 0, halves[0], halves[1]), jnp.where(far == 0, halves[1], halves[0]).astype(bf16)

    denom_sums, first, last = pl.pallas_call(
        weight_sums,
        out_shape=(sends, strip, strip),
        in_specs=[hbm] * 3,
        out_specs=(hbm,) * 3,
        scratch_shapes=[
            pltpu.SMEM(strip_bounds.shape, jnp.int32),
            pltpu.VMEM(strip.shape, bf16),
            pltpu.VMEM(strip.shape, bf16),
            pltpu.VMEM(inv_variance.shape, bf16),
            pltpu.VMEM(sends.shape, bf16),
            pltpu.SemaphoreType.DMA((row_count // CHUNK,)),
            pltpu.SemaphoreType.DMA((row_count // CHUNK,)),
            pltpu.SemaphoreType.DMA((5,)),
        ],
        name="weight_sums",
    )(strip_bounds, exposures, inv_variance)
    above = lax.ppermute(last, "patch", [(i, i + 1) for i in range(patches - 1)])
    below = lax.ppermute(first, "patch", [(i + 1, i) for i in range(patches - 1)])
    denom, denom_give = reduce_near(denom_sums)
    far_denom = lax.ppermute(denom_give, "epoch", swap)
    numer_sums = pl.pallas_call(
        weighted_sums,
        out_shape=sends,
        in_specs=[hbm] * 7,
        out_specs=hbm,
        scratch_shapes=[
            pltpu.SMEM(kernel_index.shape, jnp.int32),
            pltpu.SMEM(strip_bounds.shape, jnp.int32),
            pltpu.VMEM(basis_bank.shape, f32),
            pltpu.VMEM(strip.shape, bf16),
            pltpu.VMEM(strip.shape, bf16),
            pltpu.VMEM(sends.shape, bf16),
            pltpu.VMEM((basis_bank.shape[0], 2 * LANES), f32),
            pltpu.VMEM((exp_count, NCOMP * LANES, 2 * LANES), bf16),
            pltpu.VMEM((exp_count, UNIT, NCOMP * UNIT), bf16),
            pltpu.VMEM((exp_count, 2 * EDGE, LANES), bf16),
            pltpu.VMEM(exposures.shape, bf16),
            pltpu.VMEM(inv_variance.shape, bf16),
            pltpu.VMEM((exp_count, UNIT + 2 * EDGE, width + LANES), bf16),
            pltpu.VMEM((exp_count, NCOMP * UNIT, width), bf16),
            pltpu.VMEM((exp_count, 2 * NCOMP * EDGE, width), bf16),
            pltpu.SemaphoreType.DMA((2 * exp_count,)),
            pltpu.SemaphoreType.DMA((5,)),
            pltpu.SemaphoreType.DMA((parts,)),
        ],
        name="weighted_sums",
    )(kernel_index, strip_bounds, basis_bank, above, below, exposures, inv_variance)
    numer, numer_give = reduce_near(numer_sums)
    numer = numer + lax.ppermute(numer_give, "epoch", swap).astype(f32)
    denom = denom + far_denom.astype(f32)
    return numer / jnp.maximum(denom, 1.0), denom


def solution(mesh):
    return jax.shard_map(
        shards,
        mesh=mesh,
        in_specs=(
            P(("band", "epoch"), "patch", None),
            P(("band", "epoch"), "patch", None),
            P(("band", "epoch"), None),
            P(("band", "epoch"), None, None),
            P(),
        ),
        out_specs=(P(("band", "patch"), "epoch"), P(("band", "patch"), "epoch")),
        check_vma=False,
    )
```

```python
import jax
import jax.numpy as jnp
from jax import lax
from jax.experimental import pallas as pl
from jax.experimental.pallas import tpu as pltpu
from jax.sharding import PartitionSpec as P

UNIT = 128
HALF = 10
TAPS = 21
NCOMP = 2
LANES = 128
EDGE = 16
FAR = 2
GROUP = 4
INNER = UNIT - 2 * EDGE
TRANSPOSED = (((1,), (1,)), ((), ()))


def toeplitz(base, rows, shift):
    width = base.shape[1]
    if shift:
        base = pltpu.roll(base, shift % width, 1)
    return pltpu.roll(jnp.broadcast_to(base, (rows, width)), 0, 1, stride=1, stride_axis=0)


def matrices(index_ref, exp, taps_ref, row_ref, own_ref, edge_ref):
    lane = lax.broadcasted_iota(jnp.int32, (EDGE, LANES), 1)
    edge_top = jnp.zeros((EDGE, LANES), jnp.float32)
    edge_bottom = jnp.zeros((EDGE, LANES), jnp.float32)
    for comp in range(NCOMP):
        base = taps_ref[pl.ds(index_ref[exp, comp, 0], 1), :]
        row_ref[exp, comp * LANES : (comp + 1) * LANES, :] = toeplitz(base, LANES, 0).astype(jnp.bfloat16)
        base = taps_ref[pl.ds(index_ref[exp, comp, 1], 1), :] * (1.0 / NCOMP)
        wide = toeplitz(base, UNIT, -HALF)
        own_ref[exp, :, comp * UNIT : (comp + 1) * UNIT] = wide[:, :UNIT].astype(jnp.bfloat16)
        short = base[:, :LANES]
        first = comp * EDGE
        top = toeplitz(short, EDGE, first + EDGE - HALF)
        edge_top = jnp.where((lane >= first) & (lane < first + EDGE), top, edge_top)
        first = (NCOMP + comp) * EDGE
        bottom = toeplitz(short, EDGE, first - EDGE - HALF)
        edge_bottom = jnp.where((lane >= first) & (lane < first + EDGE), bottom, edge_bottom)
    edge_ref[exp, :EDGE, :] = edge_top.astype(jnp.bfloat16)
    edge_ref[exp, EDGE:, :] = edge_bottom.astype(jnp.bfloat16)


def mask(bounds_ref, exp, unit):
    return jnp.where((unit >= bounds_ref[exp, 0]) & (unit < bounds_ref[exp, 1]), 1.0, 0.0)


def fill_window(window_ref, exp, pixels):
    rows, width = pixels.shape
    moved = pltpu.roll(pixels, HALF, 1)
    lane = lax.broadcasted_iota(jnp.int32, (rows, LANES), 1)
    head = moved[:, :LANES]
    window_ref[exp, :, :LANES] = jnp.where(lane < HALF, 0.0, head).astype(jnp.bfloat16)
    window_ref[exp, :, LANES:width] = moved[:, LANES:].astype(jnp.bfloat16)
    window_ref[exp, :, width:] = jnp.where(lane < HALF, head, 0.0).astype(jnp.bfloat16)


def row_filter(window_ref, exp, matrix, start, count):
    stacked = jnp.concatenate(
        [window_ref[exp, :, block * LANES : (block + 2) * LANES] for block in range(start, start + count)], axis=0
    )
    return lax.dot_general(stacked, matrix, TRANSPOSED, preferred_element_type=jnp.float32).astype(jnp.bfloat16)


def start_all(pairs, sems):
    copies = [pltpu.make_async_copy(source, target, sems.at[i]) for i, (source, target) in enumerate(pairs)]
    for copy in copies:
        copy.start()
    return copies


def wait_all(copies):
    for copy in copies:
        copy.wait()


def own_sums(
    index_hbm, bounds_hbm, bank_hbm, pixels_hbm, variance_hbm,
    out_hbm, core_hbm, link_hbm, strips_hbm, row_hbm, edge_hbm,
    index_ref, bounds_ref, bank_ref, pixels_ref, variance_ref, out_ref, strips_ref, row_ref, edge_ref,
    taps_ref, own_ref, window_ref, across_ref, in_sems, out_sems,
):
    unit = lax.axis_index("patch")
    odd = lax.rem(unit, 2)
    exp_count, rows, width = pixels_ref.shape
    near, _, share = out_ref.shape
    sources = [(index_hbm, index_ref), (bank_hbm, bank_ref), (bounds_hbm, bounds_ref)]
    sources += [(pixels_hbm.at[e], pixels_ref.at[e]) for e in range(exp_count)]
    sources += [(variance_hbm.at[e], variance_ref.at[e]) for e in range(exp_count)]
    arrivals = start_all(sources, in_sems)
    wait_all(arrivals[:3])
    bank = bank_ref[...]
    bank = (bank / jnp.sum(bank, axis=1, keepdims=True)).astype(jnp.bfloat16).astype(jnp.float32)
    taps_ref[...] = jnp.concatenate([bank, jnp.zeros((bank.shape[0], 2 * LANES - TAPS), jnp.float32)], axis=1)
    for exp in range(exp_count):
        matrices(index_ref, exp, taps_ref, row_ref, own_ref, edge_ref)
    for exp in range(exp_count):
        arrivals[3 + exp].wait()
        fill_window(window_ref, exp, pixels_ref[exp].astype(jnp.float32))
        for start in range(0, width // LANES, GROUP):
            filtered = row_filter(window_ref, exp, row_ref[exp], start, GROUP)
            for block in range(GROUP):
                at = slice((start + block) * LANES, (start + block + 1) * LANES)
                for comp in range(NCOMP):
                    across_ref[exp, comp * UNIT : (comp + 1) * UNIT, at] = filtered[
                        block * UNIT : (block + 1) * UNIT, comp * LANES : (comp + 1) * LANES
                    ]
    to_core = pl.multiple_of((1 - odd) * (rows - EDGE), EDGE)
    to_link = pl.multiple_of(odd * (rows - EDGE), EDGE)
    leaves = start_all(
        [
            (pixels_ref.at[:, pl.ds(to_core, EDGE)], core_hbm),
            (pixels_ref.at[:, pl.ds(to_link, EDGE)], link_hbm),
            (row_ref, row_hbm),
            (edge_ref, edge_hbm),
        ],
        out_sems,
    )
    wait_all(arrivals[3 + exp_count :])
    masks = [mask(bounds_ref, exp, unit) for exp in range(exp_count)]
    for part in range(width // share):
        far, x = divmod(part, near)
        at = slice(part * share, (part + 1) * share)
        numer = jnp.zeros((rows, share), jnp.float32)
        denom = jnp.zeros((rows, share), jnp.float32)
        for exp in range(exp_count):
            weights = variance_ref[exp, :, at].astype(jnp.float32) * masks[exp]
            numer += weights * jnp.dot(own_ref[exp], across_ref[exp, :, at], preferred_element_type=jnp.float32)
            denom += weights
        row = far * (INNER + UNIT)
        out_ref[x, row : row + INNER, :] = numer[EDGE : UNIT - EDGE].astype(jnp.bfloat16)
        out_ref[x, row + INNER : row + INNER + UNIT, :] = denom.astype(jnp.bfloat16)
        strips_ref[:EDGE, at] = numer[:EDGE]
        strips_ref[EDGE:, at] = numer[UNIT - EDGE :]
        lines = pl.ds(row, INNER + UNIT)
        leaves.append(pltpu.make_async_copy(out_ref.at[x, lines], out_hbm.at[x, lines], out_sems.at[len(leaves)]))
        leaves[-1].start()
    leaves.append(pltpu.make_async_copy(strips_ref, strips_hbm, out_sems.at[len(leaves)]))
    leaves[-1].start()
    wait_all(leaves)


def strip_sums(
    bounds_ref, place_ref, core_ref, link_ref, top_ref, bottom_ref, strips_ref, row_ref, edge_ref,
    keep_ref, give_ref, window_ref, across_ref,
):
    unit, far = place_ref[0], place_ref[1]
    odd = lax.rem(unit, 2) == 1
    exp_count, _, width = core_ref.shape
    total = strips_ref[...]
    for exp in range(exp_count):
        core, link = core_ref[exp].astype(jnp.float32), link_ref[exp].astype(jnp.float32)
        above = jnp.where(odd, core, link) * mask(bounds_ref, exp, unit - 1)
        below = jnp.where(odd, link, core) * mask(bounds_ref, exp, unit + 1)
        fill_window(window_ref, 0, jnp.concatenate([above, below], axis=0))
        blocks = width // LANES
        filtered = row_filter(window_ref, 0, row_ref[exp], 0, blocks)
        for block in range(blocks):
            at = slice(block * LANES, (block + 1) * LANES)
            for comp in range(NCOMP):
                mine = filtered[block * 2 * EDGE : (block + 1) * 2 * EDGE, comp * LANES : (comp + 1) * LANES]
                across_ref[comp * EDGE : (comp + 1) * EDGE, at] = mine[:EDGE]
                first = (NCOMP + comp) * EDGE
                across_ref[first : first + EDGE, at] = mine[EDGE:]
        smoothed = jnp.dot(
            edge_ref[exp, :, : 2 * NCOMP * EDGE], across_ref[...], preferred_element_type=jnp.float32
        )
        weights = jnp.concatenate([top_ref[exp], bottom_ref[exp]], axis=0).astype(jnp.float32)
        total = total + weights * mask(bounds_ref, exp, unit) * smoothed
    near, _, share = keep_ref.shape
    for x in range(near):
        first = total[:, x * share : (x + 1) * share]
        second = total[:, (near + x) * share : (near + x + 1) * share]
        keep_ref[x] = jnp.where(far == 0, first, second)
        give_ref[x] = jnp.where(far == 0, second, first).astype(give_ref.dtype)


def whole(shape):
    return pl.BlockSpec(shape, lambda *_: (0,) * len(shape))


def shards(exposures, inv_variance, strip_bounds, kernel_index, basis_bank):
    exp_count, row_count, width = exposures.shape
    patches, parts = lax.axis_size("patch"), lax.axis_size("epoch")
    near = parts // FAR
    share = width // parts
    f32, bf16 = jnp.float32, jnp.bfloat16
    hbm = pl.BlockSpec(memory_space=pl.ANY)
    far = jnp.where(lax.axis_index("epoch") >= near, 1, 0)
    groups = [[y * near + x for x in range(near)] for y in range(FAR)]
    swap = [(at, (at + near) % parts) for at in range(parts)]
    lines = INNER + row_count

    def shape(*dims, dtype=bf16):
        return jax.ShapeDtypeStruct(dims, dtype)

    def vmem(struct):
        return pltpu.VMEM(struct.shape, struct.dtype)

    strip = shape(exp_count, EDGE, width)
    sends = shape(near, FAR * lines, share)
    edge_rows = shape(2 * EDGE, width, dtype=f32)
    row_mat = shape(exp_count, NCOMP * LANES, 2 * LANES)
    edge_mat = shape(exp_count, 2 * EDGE, LANES)
    sums, to_core, to_link, strips, row_mats, edge_mats = pl.pallas_call(
        own_sums,
        out_shape=(sends, strip, strip, edge_rows, row_mat, edge_mat),
        in_specs=[hbm] * 5,
        out_specs=(hbm,) * 6,
        scratch_shapes=[
            pltpu.SMEM(kernel_index.shape, jnp.int32),
            pltpu.SMEM(strip_bounds.shape, jnp.int32),
            vmem(basis_bank),
            vmem(exposures),
            vmem(inv_variance),
            vmem(sends),
            vmem(edge_rows),
            vmem(row_mat),
            vmem(edge_mat),
            pltpu.VMEM((basis_bank.shape[0], 2 * LANES), f32),
            pltpu.VMEM((exp_count, UNIT, NCOMP * UNIT), bf16),
            pltpu.VMEM((exp_count, UNIT, width + LANES), bf16),
            pltpu.VMEM((exp_count, NCOMP * UNIT, width), bf16),
            pltpu.SemaphoreType.DMA((3 + 2 * exp_count,)),
            pltpu.SemaphoreType.DMA((5 + parts,)),
        ],
        name="own_sums",
    )(kernel_index, strip_bounds, basis_bank, exposures, inv_variance)

    received = lax.all_to_all(sums, "epoch", 0, 0, tiled=True, axis_index_groups=groups)

    from_core = lax.ppermute(to_core, "patch", [(at, at ^ 1) for at in range(patches)])
    from_link = lax.ppermute(to_link, "patch", [(at, ((at + 1) ^ 1) - 1) for at in range(1, patches - 1)])
    smem = pl.BlockSpec(memory_space=pltpu.SMEM)
    place = jnp.stack([lax.axis_index("patch"), far]).astype(jnp.int32)
    strip_keep, strip_give = pl.pallas_call(
        strip_sums,
        out_shape=(shape(near, 2 * EDGE, share, dtype=f32), shape(near, 2 * EDGE, share)),
        grid=(1,),
        in_specs=[
            smem,
            smem,
            whole(strip.shape),
            whole(strip.shape),
            pl.BlockSpec(strip.shape, lambda i: (0, 0, 0)),
            pl.BlockSpec(strip.shape, lambda i: (0, row_count // EDGE - 1, 0)),
            whole(strips.shape),
            whole(row_mats.shape),
            whole(edge_mats.shape),
        ],
        out_specs=(whole((near, 2 * EDGE, share)), whole((near, 2 * EDGE, share))),
        scratch_shapes=[
            pltpu.VMEM((1, 2 * EDGE, width + LANES), bf16),
            pltpu.VMEM((2 * NCOMP * EDGE, width), bf16),
        ],
        name="strip_sums",
    )(strip_bounds, place, from_core, from_link, inv_variance, inv_variance, strips, row_mats, edge_mats)

    received, strip_give = lax.optimization_barrier((received, strip_give))
    received = received.reshape(near, FAR, lines, share)

    def half(at):
        return jnp.sum(lax.dynamic_index_in_dim(received, at, 1, keepdims=False).astype(f32), axis=0)

    keep, give = half(far), half(1 - far).astype(bf16)
    inner = keep + lax.ppermute(give, "epoch", swap).astype(f32)
    strip_sum = (strip_keep + lax.ppermute(strip_give, "epoch", swap).astype(f32)).astype(bf16)

    strip_parts = lax.all_to_all(strip_sum, "epoch", 0, 0, tiled=True, axis_index_groups=groups)
    edges = jnp.sum(strip_parts.astype(f32), axis=0)

    numer = jnp.concatenate([edges[:EDGE], inner[:INNER], edges[EDGE:]], axis=0)
    denom = inner[INNER:]
    return numer / jnp.maximum(denom, 1.0), denom


def solution(mesh):
    return jax.shard_map(
        shards,
        mesh=mesh,
        in_specs=(
            P(("band", "epoch"), "patch", None),
            P(("band", "epoch"), "patch", None),
            P(("band", "epoch"), None),
            P(("band", "epoch"), None, None),
            P(),
        ),
        out_specs=(P(("band", "patch"), "epoch"), P(("band", "patch"), "epoch")),
        check_vma=False,
    )
```

```python
import jax
import jax.numpy as jnp
from jax import lax
from jax.experimental import pallas as pl
from jax.experimental.pallas import tpu as pltpu
from jax.sharding import PartitionSpec as P

UNIT = 128
HALF = 10
TAPS = 21
NCOMP = 2
LANES = 128
EDGE = 16
FAR = 2
GROUP = 4
INNER = UNIT - 2 * EDGE
TRANSPOSED = (((1,), (1,)), ((), ()))


def toeplitz(base, rows, shift):
    width = base.shape[1]
    if shift:
        base = pltpu.roll(base, shift % width, 1)
    return pltpu.roll(jnp.broadcast_to(base, (rows, width)), 0, 1, stride=1, stride_axis=0)


def matrices(index_ref, exp, taps_ref, row_ref, own_ref, edge_ref):
    lane = lax.broadcasted_iota(jnp.int32, (EDGE, LANES), 1)
    edge_top = jnp.zeros((EDGE, LANES), jnp.float32)
    edge_bottom = jnp.zeros((EDGE, LANES), jnp.float32)
    for comp in range(NCOMP):
        base = taps_ref[pl.ds(index_ref[exp, comp, 0], 1), :]
        row_ref[exp, comp * LANES : (comp + 1) * LANES, :] = toeplitz(base, LANES, 0).astype(jnp.bfloat16)
        base = taps_ref[pl.ds(index_ref[exp, comp, 1], 1), :] * (1.0 / NCOMP)
        wide = toeplitz(base, UNIT, -HALF)
        own_ref[exp, :, comp * UNIT : (comp + 1) * UNIT] = wide[:, :UNIT].astype(jnp.bfloat16)
        short = base[:, :LANES]
        first = comp * EDGE
        top = toeplitz(short, EDGE, first + EDGE - HALF)
        edge_top = jnp.where((lane >= first) & (lane < first + EDGE), top, edge_top)
        first = (NCOMP + comp) * EDGE
        bottom = toeplitz(short, EDGE, first - EDGE - HALF)
        edge_bottom = jnp.where((lane >= first) & (lane < first + EDGE), bottom, edge_bottom)
    edge_ref[exp, :EDGE, :] = edge_top.astype(jnp.bfloat16)
    edge_ref[exp, EDGE:, :] = edge_bottom.astype(jnp.bfloat16)


def mask(bounds_ref, exp, unit):
    return jnp.where((unit >= bounds_ref[exp, 0]) & (unit < bounds_ref[exp, 1]), 1.0, 0.0)


def fill_window(window_ref, exp, pixels):
    rows, width = pixels.shape
    moved = pltpu.roll(pixels, HALF, 1)
    lane = lax.broadcasted_iota(jnp.int32, (rows, LANES), 1)
    head = moved[:, :LANES]
    window_ref[exp, :, :LANES] = jnp.where(lane < HALF, 0.0, head).astype(jnp.bfloat16)
    window_ref[exp, :, LANES:width] = moved[:, LANES:].astype(jnp.bfloat16)
    window_ref[exp, :, width:] = jnp.where(lane < HALF, head, 0.0).astype(jnp.bfloat16)


def row_filter(window_ref, exp, matrix, start, count):
    stacked = jnp.concatenate(
        [window_ref[exp, :, block * LANES : (block + 2) * LANES] for block in range(start, start + count)], axis=0
    )
    return lax.dot_general(stacked, matrix, TRANSPOSED, preferred_element_type=jnp.float32).astype(jnp.bfloat16)


def start_all(pairs, sems):
    copies = [pltpu.make_async_copy(source, target, sems.at[i]) for i, (source, target) in enumerate(pairs)]
    for copy in copies:
        copy.start()
    return copies


def wait_all(copies):
    for copy in copies:
        copy.wait()


def own_sums(
    index_hbm, bounds_hbm, bank_hbm, pixels_hbm, variance_hbm,
    out_hbm, core_hbm, link_hbm, strips_hbm, row_hbm, edge_hbm,
    index_ref, bounds_ref, bank_ref, pixels_ref, variance_ref, out_ref, strips_ref, row_ref, edge_ref,
    taps_ref, own_ref, window_ref, across_ref, in_sems, out_sems,
):
    unit = lax.axis_index("patch")
    odd = lax.rem(unit, 2)
    exp_count, rows, width = pixels_ref.shape
    near, _, share = out_ref.shape
    sources = [(index_hbm, index_ref), (bank_hbm, bank_ref), (bounds_hbm, bounds_ref)]
    sources += [(pixels_hbm.at[e], pixels_ref.at[e]) for e in range(exp_count)]
    sources += [(variance_hbm.at[e], variance_ref.at[e]) for e in range(exp_count)]
    arrivals = start_all(sources, in_sems)
    wait_all(arrivals[:3])
    bank = bank_ref[...]
    bank = (bank / jnp.sum(bank, axis=1, keepdims=True)).astype(jnp.bfloat16).astype(jnp.float32)
    taps_ref[...] = jnp.concatenate([bank, jnp.zeros((bank.shape[0], 2 * LANES - TAPS), jnp.float32)], axis=1)
    for exp in range(exp_count):
        matrices(index_ref, exp, taps_ref, row_ref, own_ref, edge_ref)
    for exp in range(exp_count):
        arrivals[3 + exp].wait()
        fill_window(window_ref, exp, pixels_ref[exp].astype(jnp.float32))
        for start in range(0, width // LANES, GROUP):
            filtered = row_filter(window_ref, exp, row_ref[exp], start, GROUP)
            for block in range(GROUP):
                at = slice((start + block) * LANES, (start + block + 1) * LANES)
                for comp in range(NCOMP):
                    across_ref[exp, comp * UNIT : (comp + 1) * UNIT, at] = filtered[
                        block * UNIT : (block + 1) * UNIT, comp * LANES : (comp + 1) * LANES
                    ]
    to_core = pl.multiple_of((1 - odd) * (rows - EDGE), EDGE)
    to_link = pl.multiple_of(odd * (rows - EDGE), EDGE)
    leaves = start_all(
        [
            (pixels_ref.at[:, pl.ds(to_core, EDGE)], core_hbm),
            (pixels_ref.at[:, pl.ds(to_link, EDGE)], link_hbm),
            (row_ref, row_hbm),
            (edge_ref, edge_hbm),
        ],
        out_sems,
    )
    wait_all(arrivals[3 + exp_count :])
    masks = [mask(bounds_ref, exp, unit) for exp in range(exp_count)]
    for part in range(width // share):
        far, x = divmod(part, near)
        at = slice(part * share, (part + 1) * share)
        numer = jnp.zeros((rows, share), jnp.float32)
        denom = jnp.zeros((rows, share), jnp.float32)
        for exp in range(exp_count):
            weights = variance_ref[exp, :, at].astype(jnp.float32) * masks[exp]
            numer += weights * jnp.dot(own_ref[exp], across_ref[exp, :, at], preferred_element_type=jnp.float32)
            denom += weights
        row = far * (INNER + UNIT)
        out_ref[x, row : row + INNER, :] = numer[EDGE : UNIT - EDGE].astype(jnp.bfloat16)
        out_ref[x, row + INNER : row + INNER + UNIT, :] = denom.astype(jnp.bfloat16)
        strips_ref[:EDGE, at] = numer[:EDGE]
        strips_ref[EDGE:, at] = numer[UNIT - EDGE :]
        lines = pl.ds(row, INNER + UNIT)
        leaves.append(pltpu.make_async_copy(out_ref.at[x, lines], out_hbm.at[x, lines], out_sems.at[len(leaves)]))
        leaves[-1].start()
    leaves.append(pltpu.make_async_copy(strips_ref, strips_hbm, out_sems.at[len(leaves)]))
    leaves[-1].start()
    wait_all(leaves)


def strip_sums(
    bounds_hbm, core_ref, link_ref, variance_hbm, strips_hbm, row_hbm, edge_hbm,
    keep_ref, give_ref,
    bounds_ref, top_ref, bottom_ref, strips_ref, row_ref, edge_ref,
    window_ref, across_ref, in_sems,
):
    unit = lax.axis_index("patch")
    odd = lax.rem(unit, 2) == 1
    exp_count, _, width = core_ref.shape
    near, _, share = keep_ref.shape
    rows = variance_hbm.shape[1]
    far = lax.axis_index("epoch") >= near
    wait_all(
        start_all(
            [
                (bounds_hbm, bounds_ref),
                (row_hbm, row_ref),
                (edge_hbm, edge_ref),
                (strips_hbm, strips_ref),
                (variance_hbm.at[:, pl.ds(0, EDGE)], top_ref),
                (variance_hbm.at[:, pl.ds(rows - EDGE, EDGE)], bottom_ref),
            ],
            in_sems,
        )
    )
    total = strips_ref[...]
    for exp in range(exp_count):
        core, link = core_ref[exp].astype(jnp.float32), link_ref[exp].astype(jnp.float32)
        above = jnp.where(odd, core, link) * mask(bounds_ref, exp, unit - 1)
        below = jnp.where(odd, link, core) * mask(bounds_ref, exp, unit + 1)
        fill_window(window_ref, exp, jnp.concatenate([above, below], axis=0))
        blocks = width // LANES
        filtered = row_filter(window_ref, exp, row_ref[exp], 0, blocks)
        for block in range(blocks):
            at = slice(block * LANES, (block + 1) * LANES)
            for comp in range(NCOMP):
                mine = filtered[block * 2 * EDGE : (block + 1) * 2 * EDGE, comp * LANES : (comp + 1) * LANES]
                across_ref[exp, comp * EDGE : (comp + 1) * EDGE, at] = mine[:EDGE]
                first = (NCOMP + comp) * EDGE
                across_ref[exp, first : first + EDGE, at] = mine[EDGE:]
        smoothed = jnp.dot(
            edge_ref[exp, :, : 2 * NCOMP * EDGE], across_ref[exp], preferred_element_type=jnp.float32
        )
        weights = jnp.concatenate([top_ref[exp], bottom_ref[exp]], axis=0).astype(jnp.float32)
        total = total + weights * mask(bounds_ref, exp, unit) * smoothed
    for x in range(near):
        first = total[:, x * share : (x + 1) * share]
        second = total[:, (near + x) * share : (near + x + 1) * share]
        keep_ref[x] = jnp.where(far, second, first)
        give_ref[x] = jnp.where(far, first, second).astype(give_ref.dtype)


def shards(exposures, inv_variance, strip_bounds, kernel_index, basis_bank):
    exp_count, row_count, width = exposures.shape
    patches, parts = lax.axis_size("patch"), lax.axis_size("epoch")
    near = parts // FAR
    share = width // parts
    f32, bf16 = jnp.float32, jnp.bfloat16
    hbm = pl.BlockSpec(memory_space=pl.ANY)
    far = jnp.where(lax.axis_index("epoch") >= near, 1, 0)
    groups = [[y * near + x for x in range(near)] for y in range(FAR)]
    swap = [(at, (at + near) % parts) for at in range(parts)]
    lines = INNER + row_count

    def shape(*dims, dtype=bf16):
        return jax.ShapeDtypeStruct(dims, dtype)

    def vmem(struct):
        return pltpu.VMEM(struct.shape, struct.dtype)

    strip = shape(exp_count, EDGE, width)
    sends = shape(near, FAR * lines, share)
    edge_rows = shape(2 * EDGE, width, dtype=f32)
    row_mat = shape(exp_count, NCOMP * LANES, 2 * LANES)
    edge_mat = shape(exp_count, 2 * EDGE, LANES)
    sums, to_core, to_link, strips, row_mats, edge_mats = pl.pallas_call(
        own_sums,
        out_shape=(sends, strip, strip, edge_rows, row_mat, edge_mat),
        in_specs=[hbm] * 5,
        out_specs=(hbm,) * 6,
        scratch_shapes=[
            pltpu.SMEM(kernel_index.shape, jnp.int32),
            pltpu.SMEM(strip_bounds.shape, jnp.int32),
            vmem(basis_bank),
            vmem(exposures),
            vmem(inv_variance),
            vmem(sends),
            vmem(edge_rows),
            vmem(row_mat),
            vmem(edge_mat),
            pltpu.VMEM((basis_bank.shape[0], 2 * LANES), f32),
            pltpu.VMEM((exp_count, UNIT, NCOMP * UNIT), bf16),
            pltpu.VMEM((exp_count, UNIT, width + LANES), bf16),
            pltpu.VMEM((exp_count, NCOMP * UNIT, width), bf16),
            pltpu.SemaphoreType.DMA((3 + 2 * exp_count,)),
            pltpu.SemaphoreType.DMA((5 + parts,)),
        ],
        name="own_sums",
    )(kernel_index, strip_bounds, basis_bank, exposures, inv_variance)

    received = lax.all_to_all(sums, "epoch", 0, 0, tiled=True, axis_index_groups=groups)

    from_core = lax.ppermute(to_core, "patch", [(at, at ^ 1) for at in range(patches)])
    from_link = lax.ppermute(to_link, "patch", [(at, ((at + 1) ^ 1) - 1) for at in range(1, patches - 1)])
    keep_shape, give_shape = shape(near, 2 * EDGE, share, dtype=f32), shape(near, 2 * EDGE, share)
    vmem_spec = pl.BlockSpec(memory_space=pltpu.VMEM)
    strip_keep, strip_give = pl.pallas_call(
        strip_sums,
        out_shape=(keep_shape, give_shape),
        in_specs=[hbm, vmem_spec, vmem_spec, hbm, hbm, hbm, hbm],
        out_specs=(vmem_spec,) * 2,
        scratch_shapes=[
            pltpu.SMEM(strip_bounds.shape, jnp.int32),
            *[vmem(strip)] * 2,
            vmem(edge_rows),
            vmem(row_mat),
            vmem(edge_mat),
            pltpu.VMEM((exp_count, 2 * EDGE, width + LANES), bf16),
            pltpu.VMEM((exp_count, 2 * NCOMP * EDGE, width), bf16),
            pltpu.SemaphoreType.DMA((6,)),
        ],
        compiler_params=pltpu.CompilerParams(vmem_limit_bytes=12 * 1024 * 1024),
        name="strip_sums",
    )(strip_bounds, from_core, from_link, inv_variance, strips, row_mats, edge_mats)
    received, strip_give = lax.optimization_barrier((received, strip_give))
    received = received.reshape(near, FAR, lines, share)

    def half(at):
        return jnp.sum(lax.dynamic_index_in_dim(received, at, 1, keepdims=False).astype(f32), axis=0)

    keep, give = half(far), half(1 - far).astype(bf16)
    inner = keep + lax.ppermute(give, "epoch", swap).astype(f32)
    strip_sum = (strip_keep + lax.ppermute(strip_give, "epoch", swap).astype(f32)).astype(bf16)

    strip_parts = lax.all_to_all(strip_sum, "epoch", 0, 0, tiled=True, axis_index_groups=groups)
    edges = jnp.sum(strip_parts.astype(f32), axis=0)

    numer = jnp.concatenate([edges[:EDGE], inner[:INNER], edges[EDGE:]], axis=0)
    denom = inner[INNER:]
    return numer / jnp.maximum(denom, 1.0), denom


def solution(mesh):
    return jax.shard_map(
        shards,
        mesh=mesh,
        in_specs=(
            P(("band", "epoch"), "patch", None),
            P(("band", "epoch"), "patch", None),
            P(("band", "epoch"), None),
            P(("band", "epoch"), None, None),
            P(),
        ),
        out_specs=(P(("band", "patch"), "epoch"), P(("band", "patch"), "epoch")),
        check_vma=False,
    )
```

```python
import jax
import jax.numpy as jnp
from jax import lax
from jax.experimental import pallas as pl
from jax.experimental.pallas import tpu as pltpu
from jax.sharding import PartitionSpec as P

UNIT = 128
HALF = 10
TAPS = 21
NCOMP = 2
LANES = 128
EDGE = 16
FAR = 2
GROUP = 4
INNER = UNIT - 2 * EDGE
TRANSPOSED = (((1,), (1,)), ((), ()))


def toeplitz(base, rows, shift):
    width = base.shape[1]
    if shift:
        base = pltpu.roll(base, shift % width, 1)
    return pltpu.roll(jnp.broadcast_to(base, (rows, width)), 0, 1, stride=1, stride_axis=0)


def matrices(index_ref, exp, covers, taps_ref, row_ref, own_ref, edge_ref):
    lane = lax.broadcasted_iota(jnp.int32, (EDGE, LANES), 1)
    edge_top = jnp.zeros((EDGE, LANES), jnp.float32)
    edge_bottom = jnp.zeros((EDGE, LANES), jnp.float32)
    for comp in range(NCOMP):
        base = taps_ref[pl.ds(index_ref[exp, comp, 0], 1), :]
        row_ref[exp, comp * LANES : (comp + 1) * LANES, :] = toeplitz(base, LANES, 0).astype(jnp.bfloat16)
        base = taps_ref[pl.ds(index_ref[exp, comp, 1], 1), :] * (1.0 / NCOMP)
        wide = toeplitz(base, UNIT, -HALF)
        own_ref[exp, :, comp * UNIT : (comp + 1) * UNIT] = wide[:, :UNIT].astype(jnp.bfloat16)
        short = base[:, :LANES]
        first = comp * EDGE
        top = toeplitz(short, EDGE, first + EDGE - HALF)
        edge_top = jnp.where((lane >= first) & (lane < first + EDGE), top, edge_top)
        first = (NCOMP + comp) * EDGE
        bottom = toeplitz(short, EDGE, first - EDGE - HALF)
        edge_bottom = jnp.where((lane >= first) & (lane < first + EDGE), bottom, edge_bottom)
    edge_ref[exp, :EDGE, :] = (edge_top * (covers[0] * covers[1])).astype(jnp.bfloat16)
    edge_ref[exp, EDGE:, :] = (edge_bottom * (covers[1] * covers[2])).astype(jnp.bfloat16)


def mask(bounds_ref, exp, unit):
    return jnp.where((unit >= bounds_ref[exp, 0]) & (unit < bounds_ref[exp, 1]), 1.0, 0.0)


def fill_window(window_ref, exp, pixels):
    rows, width = pixels.shape
    moved = pltpu.roll(pixels, HALF, 1)
    lane = lax.broadcasted_iota(jnp.int32, (rows, LANES), 1)
    head = moved[:, :LANES]
    window_ref[exp, :, :LANES] = jnp.where(lane < HALF, 0.0, head).astype(jnp.bfloat16)
    window_ref[exp, :, LANES:width] = moved[:, LANES:].astype(jnp.bfloat16)
    window_ref[exp, :, width:] = jnp.where(lane < HALF, head, 0.0).astype(jnp.bfloat16)


def row_filter(window_ref, exp, matrix, start, count):
    stacked = jnp.concatenate(
        [window_ref[exp, :, block * LANES : (block + 2) * LANES] for block in range(start, start + count)], axis=0
    )
    return lax.dot_general(stacked, matrix, TRANSPOSED, preferred_element_type=jnp.float32).astype(jnp.bfloat16)


def start_all(pairs, sems):
    copies = [pltpu.make_async_copy(source, target, sems.at[i]) for i, (source, target) in enumerate(pairs)]
    for copy in copies:
        copy.start()
    return copies


def wait_all(copies):
    for copy in copies:
        copy.wait()


def own_sums(
    index_hbm, bounds_hbm, bank_hbm, pixels_hbm, variance_hbm,
    out_hbm, core_hbm, link_hbm, strips_hbm, row_hbm, edge_hbm,
    index_ref, bounds_ref, bank_ref, pixels_ref, variance_ref, out_ref, strips_ref, row_ref, edge_ref,
    taps_ref, own_ref, window_ref, across_ref, in_sems, out_sems,
):
    unit = lax.axis_index("patch")
    odd = lax.rem(unit, 2)
    exp_count, rows, width = pixels_ref.shape
    near, _, share = out_ref.shape
    sources = [(index_hbm, index_ref), (bank_hbm, bank_ref), (bounds_hbm, bounds_ref)]
    sources += [(pixels_hbm.at[e], pixels_ref.at[e]) for e in range(exp_count)]
    sources += [(variance_hbm.at[e], variance_ref.at[e]) for e in range(exp_count)]
    arrivals = start_all(sources, in_sems)
    wait_all(arrivals[:3])
    bank = bank_ref[...]
    bank = (bank / jnp.sum(bank, axis=1, keepdims=True)).astype(jnp.bfloat16).astype(jnp.float32)
    taps_ref[...] = jnp.concatenate([bank, jnp.zeros((bank.shape[0], 2 * LANES - TAPS), jnp.float32)], axis=1)
    for exp in range(exp_count):
        covers = [mask(bounds_ref, exp, unit + step) for step in (-1, 0, 1)]
        matrices(index_ref, exp, covers, taps_ref, row_ref, own_ref, edge_ref)
    for exp in range(exp_count):
        arrivals[3 + exp].wait()
        fill_window(window_ref, exp, pixels_ref[exp].astype(jnp.float32))
        for start in range(0, width // LANES, GROUP):
            filtered = row_filter(window_ref, exp, row_ref[exp], start, GROUP)
            for block in range(GROUP):
                at = slice((start + block) * LANES, (start + block + 1) * LANES)
                for comp in range(NCOMP):
                    across_ref[exp, comp * UNIT : (comp + 1) * UNIT, at] = filtered[
                        block * UNIT : (block + 1) * UNIT, comp * LANES : (comp + 1) * LANES
                    ]
    to_core = pl.multiple_of((1 - odd) * (rows - EDGE), EDGE)
    to_link = pl.multiple_of(odd * (rows - EDGE), EDGE)
    leaves = start_all(
        [
            (pixels_ref.at[:, pl.ds(to_core, EDGE)], core_hbm),
            (pixels_ref.at[:, pl.ds(to_link, EDGE)], link_hbm),
            (row_ref, row_hbm),
            (edge_ref, edge_hbm),
        ],
        out_sems,
    )
    wait_all(arrivals[3 + exp_count :])
    masks = [mask(bounds_ref, exp, unit) for exp in range(exp_count)]
    for part in range(width // share):
        far, x = divmod(part, near)
        at = slice(part * share, (part + 1) * share)
        numer = jnp.zeros((rows, share), jnp.float32)
        denom = jnp.zeros((rows, share), jnp.float32)
        for exp in range(exp_count):
            weights = variance_ref[exp, :, at].astype(jnp.float32) * masks[exp]
            numer += weights * jnp.dot(own_ref[exp], across_ref[exp, :, at], preferred_element_type=jnp.float32)
            denom += weights
        row = far * (INNER + UNIT)
        out_ref[x, row : row + INNER, :] = numer[EDGE : UNIT - EDGE].astype(jnp.bfloat16)
        out_ref[x, row + INNER : row + INNER + UNIT, :] = denom.astype(jnp.bfloat16)
        strips_ref[:EDGE, at] = numer[:EDGE]
        strips_ref[EDGE:, at] = numer[UNIT - EDGE :]
        lines = pl.ds(row, INNER + UNIT)
        leaves.append(pltpu.make_async_copy(out_ref.at[x, lines], out_hbm.at[x, lines], out_sems.at[len(leaves)]))
        leaves[-1].start()
    leaves.append(pltpu.make_async_copy(strips_ref, strips_hbm, out_sems.at[len(leaves)]))
    leaves[-1].start()
    wait_all(leaves)


def strip_sums(
    core_ref, link_ref, variance_hbm, strips_hbm, row_hbm, edge_hbm,
    keep_ref, give_ref,
    top_ref, bottom_ref, strips_ref, row_ref, edge_ref,
    window_ref, across_ref, in_sems,
):
    unit = lax.axis_index("patch")
    odd = lax.rem(unit, 2) == 1
    exp_count, _, width = core_ref.shape
    near, _, share = keep_ref.shape
    rows = variance_hbm.shape[1]
    far = lax.axis_index("epoch") >= near
    wait_all(
        start_all(
            [
                (row_hbm, row_ref),
                (edge_hbm, edge_ref),
                (strips_hbm, strips_ref),
                (variance_hbm.at[:, pl.ds(0, EDGE)], top_ref),
                (variance_hbm.at[:, pl.ds(rows - EDGE, EDGE)], bottom_ref),
            ],
            in_sems,
        )
    )
    total = strips_ref[...]
    for exp in range(exp_count):
        core, link = core_ref[exp].astype(jnp.float32), link_ref[exp].astype(jnp.float32)
        above = jnp.where(odd, core, link)
        below = jnp.where(odd, link, core)
        fill_window(window_ref, exp, jnp.concatenate([above, below], axis=0))
        blocks = width // LANES
        filtered = row_filter(window_ref, exp, row_ref[exp], 0, blocks)
        for block in range(blocks):
            at = slice(block * LANES, (block + 1) * LANES)
            for comp in range(NCOMP):
                mine = filtered[block * 2 * EDGE : (block + 1) * 2 * EDGE, comp * LANES : (comp + 1) * LANES]
                across_ref[exp, comp * EDGE : (comp + 1) * EDGE, at] = mine[:EDGE]
                first = (NCOMP + comp) * EDGE
                across_ref[exp, first : first + EDGE, at] = mine[EDGE:]
        smoothed = jnp.dot(
            edge_ref[exp, :, : 2 * NCOMP * EDGE], across_ref[exp], preferred_element_type=jnp.float32
        )
        weights = jnp.concatenate([top_ref[exp], bottom_ref[exp]], axis=0).astype(jnp.float32)
        total = total + weights * smoothed
    for x in range(near):
        first = total[:, x * share : (x + 1) * share]
        second = total[:, (near + x) * share : (near + x + 1) * share]
        keep_ref[x] = jnp.where(far, second, first)
        give_ref[x] = jnp.where(far, first, second).astype(give_ref.dtype)


def shards(exposures, inv_variance, strip_bounds, kernel_index, basis_bank):
    exp_count, row_count, width = exposures.shape
    patches, parts = lax.axis_size("patch"), lax.axis_size("epoch")
    near = parts // FAR
    share = width // parts
    f32, bf16 = jnp.float32, jnp.bfloat16
    hbm = pl.BlockSpec(memory_space=pl.ANY)
    far = jnp.where(lax.axis_index("epoch") >= near, 1, 0)
    groups = [[y * near + x for x in range(near)] for y in range(FAR)]
    swap = [(at, (at + near) % parts) for at in range(parts)]
    lines = INNER + row_count

    def shape(*dims, dtype=bf16):
        return jax.ShapeDtypeStruct(dims, dtype)

    def vmem(struct):
        return pltpu.VMEM(struct.shape, struct.dtype)

    strip = shape(exp_count, EDGE, width)
    sends = shape(near, FAR * lines, share)
    edge_rows = shape(2 * EDGE, width, dtype=f32)
    row_mat = shape(exp_count, NCOMP * LANES, 2 * LANES)
    edge_mat = shape(exp_count, 2 * EDGE, LANES)
    sums, to_core, to_link, strips, row_mats, edge_mats = pl.pallas_call(
        own_sums,
        out_shape=(sends, strip, strip, edge_rows, row_mat, edge_mat),
        in_specs=[hbm] * 5,
        out_specs=(hbm,) * 6,
        scratch_shapes=[
            pltpu.SMEM(kernel_index.shape, jnp.int32),
            pltpu.SMEM(strip_bounds.shape, jnp.int32),
            vmem(basis_bank),
            vmem(exposures),
            vmem(inv_variance),
            vmem(sends),
            vmem(edge_rows),
            vmem(row_mat),
            vmem(edge_mat),
            pltpu.VMEM((basis_bank.shape[0], 2 * LANES), f32),
            pltpu.VMEM((exp_count, UNIT, NCOMP * UNIT), bf16),
            pltpu.VMEM((exp_count, UNIT, width + LANES), bf16),
            pltpu.VMEM((exp_count, NCOMP * UNIT, width), bf16),
            pltpu.SemaphoreType.DMA((3 + 2 * exp_count,)),
            pltpu.SemaphoreType.DMA((5 + parts,)),
        ],
        name="own_sums",
    )(kernel_index, strip_bounds, basis_bank, exposures, inv_variance)

    received = lax.all_to_all(sums, "epoch", 0, 0, tiled=True, axis_index_groups=groups)

    from_core = lax.ppermute(to_core, "patch", [(at, at ^ 1) for at in range(patches)])
    from_link = lax.ppermute(to_link, "patch", [(at, ((at + 1) ^ 1) - 1) for at in range(1, patches - 1)])
    keep_shape, give_shape = shape(near, 2 * EDGE, share, dtype=f32), shape(near, 2 * EDGE, share)
    vmem_spec = pl.BlockSpec(memory_space=pltpu.VMEM)
    strip_keep, strip_give = pl.pallas_call(
        strip_sums,
        out_shape=(keep_shape, give_shape),
        in_specs=[vmem_spec, vmem_spec, hbm, hbm, hbm, hbm],
        out_specs=(vmem_spec,) * 2,
        scratch_shapes=[
            *[vmem(strip)] * 2,
            vmem(edge_rows),
            vmem(row_mat),
            vmem(edge_mat),
            pltpu.VMEM((exp_count, 2 * EDGE, width + LANES), bf16),
            pltpu.VMEM((exp_count, 2 * NCOMP * EDGE, width), bf16),
            pltpu.SemaphoreType.DMA((5,)),
        ],
        compiler_params=pltpu.CompilerParams(vmem_limit_bytes=12 * 1024 * 1024),
        name="strip_sums",
    )(from_core, from_link, inv_variance, strips, row_mats, edge_mats)
    received, strip_give = lax.optimization_barrier((received, strip_give))
    received = received.reshape(near, FAR, lines, share)

    def half(at):
        return jnp.sum(lax.dynamic_index_in_dim(received, at, 1, keepdims=False).astype(f32), axis=0)

    keep, give = half(far), half(1 - far).astype(bf16)
    inner = keep + lax.ppermute(give, "epoch", swap).astype(f32)
    strip_sum = (strip_keep + lax.ppermute(strip_give, "epoch", swap).astype(f32)).astype(bf16)

    strip_parts = lax.all_to_all(strip_sum, "epoch", 0, 0, tiled=True, axis_index_groups=groups)
    edges = jnp.sum(strip_parts.astype(f32), axis=0)

    numer = jnp.concatenate([edges[:EDGE], inner[:INNER], edges[EDGE:]], axis=0)
    denom = inner[INNER:]
    return numer / jnp.maximum(denom, 1.0), denom


def solution(mesh):
    return jax.shard_map(
        shards,
        mesh=mesh,
        in_specs=(
            P(("band", "epoch"), "patch", None),
            P(("band", "epoch"), "patch", None),
            P(("band", "epoch"), None),
            P(("band", "epoch"), None, None),
            P(),
        ),
        out_specs=(P(("band", "patch"), "epoch"), P(("band", "patch"), "epoch")),
        check_vma=False,
    )
```

```python
import jax
import jax.numpy as jnp
from jax import lax
from jax.experimental import pallas as pl
from jax.experimental.pallas import tpu as pltpu
from jax.sharding import PartitionSpec as P

UNIT = 128
HALF = 10
TAPS = 21
NCOMP = 2
LANES = 128
EDGE = 16
FAR = 2
GROUP = 4
INNER = UNIT - 2 * EDGE
TRANSPOSED = (((1,), (1,)), ((), ()))


def toeplitz(base, rows, shift):
    width = base.shape[1]
    if shift:
        base = pltpu.roll(base, shift % width, 1)
    return pltpu.roll(jnp.broadcast_to(base, (rows, width)), 0, 1, stride=1, stride_axis=0)


def matrices(index_ref, exp, covers, taps_ref, row_ref, own_ref, edge_ref):
    lane = lax.broadcasted_iota(jnp.int32, (EDGE, LANES), 1)
    edge_top = jnp.zeros((EDGE, LANES), jnp.float32)
    edge_bottom = jnp.zeros((EDGE, LANES), jnp.float32)
    for comp in range(NCOMP):
        base = taps_ref[pl.ds(index_ref[exp, comp, 0], 1), :]
        row_ref[exp, comp * LANES : (comp + 1) * LANES, :] = toeplitz(base, LANES, 0).astype(jnp.bfloat16)
        base = taps_ref[pl.ds(index_ref[exp, comp, 1], 1), :] * (1.0 / NCOMP)
        wide = toeplitz(base, UNIT, -HALF)
        own_ref[exp, :, comp * UNIT : (comp + 1) * UNIT] = wide[:, :UNIT].astype(jnp.bfloat16)
        short = base[:, :LANES]
        first = comp * EDGE
        top = toeplitz(short, EDGE, first + EDGE - HALF)
        edge_top = jnp.where((lane >= first) & (lane < first + EDGE), top, edge_top)
        first = (NCOMP + comp) * EDGE
        bottom = toeplitz(short, EDGE, first - EDGE - HALF)
        edge_bottom = jnp.where((lane >= first) & (lane < first + EDGE), bottom, edge_bottom)
    edge_ref[exp, :EDGE, :] = (edge_top * (covers[0] * covers[1])).astype(jnp.bfloat16)
    edge_ref[exp, EDGE:, :] = (edge_bottom * (covers[1] * covers[2])).astype(jnp.bfloat16)


def mask(bounds_ref, exp, unit):
    return jnp.where((unit >= bounds_ref[exp, 0]) & (unit < bounds_ref[exp, 1]), 1.0, 0.0)


def fill_window(window_ref, exp, pixels):
    rows, width = pixels.shape
    moved = pltpu.roll(pixels, HALF, 1)
    lane = lax.broadcasted_iota(jnp.int32, (rows, LANES), 1)
    head = moved[:, :LANES]
    window_ref[exp, :, :LANES] = jnp.where(lane < HALF, 0.0, head).astype(jnp.bfloat16)
    window_ref[exp, :, LANES:width] = moved[:, LANES:].astype(jnp.bfloat16)
    window_ref[exp, :, width:] = jnp.where(lane < HALF, head, 0.0).astype(jnp.bfloat16)


def row_filter(window_ref, exp, matrix, start, count):
    stacked = jnp.concatenate(
        [window_ref[exp, :, block * LANES : (block + 2) * LANES] for block in range(start, start + count)], axis=0
    )
    return lax.dot_general(stacked, matrix, TRANSPOSED, preferred_element_type=jnp.float32).astype(jnp.bfloat16)


def start_all(pairs, sems):
    copies = [pltpu.make_async_copy(source, target, sems.at[i]) for i, (source, target) in enumerate(pairs)]
    for copy in copies:
        copy.start()
    return copies


def wait_all(copies):
    for copy in copies:
        copy.wait()


def own_sums(
    index_hbm, bounds_hbm, bank_hbm, pixels_hbm, variance_hbm,
    out_hbm, core_hbm, link_hbm, strips_hbm, row_hbm, edge_hbm,
    index_ref, bounds_ref, bank_ref, pixels_ref, variance_ref, out_ref, strips_ref, row_ref, edge_ref,
    taps_ref, own_ref, window_ref, across_ref, in_sems, out_sems,
):
    unit = lax.axis_index("patch")
    odd = lax.rem(unit, 2)
    exp_count, rows, width = pixels_ref.shape
    near, _, share = out_ref.shape
    sources = [(index_hbm, index_ref), (bank_hbm, bank_ref), (bounds_hbm, bounds_ref)]
    sources += [(pixels_hbm.at[e], pixels_ref.at[e]) for e in range(exp_count)]
    sources += [(variance_hbm.at[e], variance_ref.at[e]) for e in range(exp_count)]
    arrivals = start_all(sources, in_sems)
    wait_all(arrivals[:3])
    bank = bank_ref[...]
    bank = (bank / jnp.sum(bank, axis=1, keepdims=True)).astype(jnp.bfloat16).astype(jnp.float32)
    taps_ref[...] = jnp.concatenate([bank, jnp.zeros((bank.shape[0], 2 * LANES - TAPS), jnp.float32)], axis=1)
    for exp in range(exp_count):
        covers = [mask(bounds_ref, exp, unit + step) for step in (-1, 0, 1)]
        matrices(index_ref, exp, covers, taps_ref, row_ref, own_ref, edge_ref)
    wait_all(arrivals[3 : 3 + exp_count])
    to_core = pl.multiple_of((1 - odd) * (rows - EDGE), EDGE)
    to_link = pl.multiple_of(odd * (rows - EDGE), EDGE)
    leaves = start_all(
        [
            (pixels_ref.at[:, pl.ds(to_core, EDGE)], core_hbm),
            (pixels_ref.at[:, pl.ds(to_link, EDGE)], link_hbm),
            (row_ref, row_hbm),
            (edge_ref, edge_hbm),
        ],
        out_sems,
    )
    for exp in range(exp_count):
        fill_window(window_ref, exp, pixels_ref[exp].astype(jnp.float32))
        for start in range(0, width // LANES, GROUP):
            filtered = row_filter(window_ref, exp, row_ref[exp], start, GROUP)
            for block in range(GROUP):
                at = slice((start + block) * LANES, (start + block + 1) * LANES)
                for comp in range(NCOMP):
                    across_ref[exp, comp * UNIT : (comp + 1) * UNIT, at] = filtered[
                        block * UNIT : (block + 1) * UNIT, comp * LANES : (comp + 1) * LANES
                    ]
    wait_all(arrivals[3 + exp_count :])
    masks = [mask(bounds_ref, exp, unit) for exp in range(exp_count)]
    for part in range(width // share):
        far, x = divmod(part, near)
        at = slice(part * share, (part + 1) * share)
        numer = jnp.zeros((rows, share), jnp.float32)
        denom = jnp.zeros((rows, share), jnp.float32)
        for exp in range(exp_count):
            weights = variance_ref[exp, :, at].astype(jnp.float32) * masks[exp]
            numer += weights * jnp.dot(own_ref[exp], across_ref[exp, :, at], preferred_element_type=jnp.float32)
            denom += weights
        row = far * (INNER + UNIT)
        out_ref[x, row : row + INNER, :] = numer[EDGE : UNIT - EDGE].astype(jnp.bfloat16)
        out_ref[x, row + INNER : row + INNER + UNIT, :] = denom.astype(jnp.bfloat16)
        strips_ref[:EDGE, at] = numer[:EDGE]
        strips_ref[EDGE:, at] = numer[UNIT - EDGE :]
        lines = pl.ds(row, INNER + UNIT)
        leaves.append(pltpu.make_async_copy(out_ref.at[x, lines], out_hbm.at[x, lines], out_sems.at[len(leaves)]))
        leaves[-1].start()
    leaves.append(pltpu.make_async_copy(strips_ref, strips_hbm, out_sems.at[len(leaves)]))
    leaves[-1].start()
    wait_all(leaves)


def strip_sums(
    core_ref, link_ref, variance_hbm, strips_hbm, row_hbm, edge_hbm,
    keep_ref, give_ref,
    top_ref, bottom_ref, strips_ref, row_ref, edge_ref,
    window_ref, across_ref, in_sems,
):
    unit = lax.axis_index("patch")
    odd = lax.rem(unit, 2) == 1
    exp_count, _, width = core_ref.shape
    near, _, share = keep_ref.shape
    rows = variance_hbm.shape[1]
    far = lax.axis_index("epoch") >= near
    wait_all(
        start_all(
            [
                (row_hbm, row_ref),
                (edge_hbm, edge_ref),
                (strips_hbm, strips_ref),
                (variance_hbm.at[:, pl.ds(0, EDGE)], top_ref),
                (variance_hbm.at[:, pl.ds(rows - EDGE, EDGE)], bottom_ref),
            ],
            in_sems,
        )
    )
    total = strips_ref[...]
    for exp in range(exp_count):
        core, link = core_ref[exp].astype(jnp.float32), link_ref[exp].astype(jnp.float32)
        above = jnp.where(odd, core, link)
        below = jnp.where(odd, link, core)
        fill_window(window_ref, exp, jnp.concatenate([above, below], axis=0))
        blocks = width // LANES
        filtered = row_filter(window_ref, exp, row_ref[exp], 0, blocks)
        for block in range(blocks):
            at = slice(block * LANES, (block + 1) * LANES)
            for comp in range(NCOMP):
                mine = filtered[block * 2 * EDGE : (block + 1) * 2 * EDGE, comp * LANES : (comp + 1) * LANES]
                across_ref[exp, comp * EDGE : (comp + 1) * EDGE, at] = mine[:EDGE]
                first = (NCOMP + comp) * EDGE
                across_ref[exp, first : first + EDGE, at] = mine[EDGE:]
        smoothed = jnp.dot(
            edge_ref[exp, :, : 2 * NCOMP * EDGE], across_ref[exp], preferred_element_type=jnp.float32
        )
        weights = jnp.concatenate([top_ref[exp], bottom_ref[exp]], axis=0).astype(jnp.float32)
        total = total + weights * smoothed
    for x in range(near):
        first = total[:, x * share : (x + 1) * share]
        second = total[:, (near + x) * share : (near + x + 1) * share]
        keep_ref[x] = jnp.where(far, second, first)
        give_ref[x] = jnp.where(far, first, second).astype(give_ref.dtype)


def shards(exposures, inv_variance, strip_bounds, kernel_index, basis_bank):
    exp_count, row_count, width = exposures.shape
    patches, parts = lax.axis_size("patch"), lax.axis_size("epoch")
    near = parts // FAR
    share = width // parts
    f32, bf16 = jnp.float32, jnp.bfloat16
    hbm = pl.BlockSpec(memory_space=pl.ANY)
    far = jnp.where(lax.axis_index("epoch") >= near, 1, 0)
    groups = [[y * near + x for x in range(near)] for y in range(FAR)]
    swap = [(at, (at + near) % parts) for at in range(parts)]
    lines = INNER + row_count

    def shape(*dims, dtype=bf16):
        return jax.ShapeDtypeStruct(dims, dtype)

    def vmem(struct):
        return pltpu.VMEM(struct.shape, struct.dtype)

    strip = shape(exp_count, EDGE, width)
    sends = shape(near, FAR * lines, share)
    edge_rows = shape(2 * EDGE, width, dtype=f32)
    row_mat = shape(exp_count, NCOMP * LANES, 2 * LANES)
    edge_mat = shape(exp_count, 2 * EDGE, LANES)
    sums, to_core, to_link, strips, row_mats, edge_mats = pl.pallas_call(
        own_sums,
        out_shape=(sends, strip, strip, edge_rows, row_mat, edge_mat),
        in_specs=[hbm] * 5,
        out_specs=(hbm,) * 6,
        scratch_shapes=[
            pltpu.SMEM(kernel_index.shape, jnp.int32),
            pltpu.SMEM(strip_bounds.shape, jnp.int32),
            vmem(basis_bank),
            vmem(exposures),
            vmem(inv_variance),
            vmem(sends),
            vmem(edge_rows),
            vmem(row_mat),
            vmem(edge_mat),
            pltpu.VMEM((basis_bank.shape[0], 2 * LANES), f32),
            pltpu.VMEM((exp_count, UNIT, NCOMP * UNIT), bf16),
            pltpu.VMEM((exp_count, UNIT, width + LANES), bf16),
            pltpu.VMEM((exp_count, NCOMP * UNIT, width), bf16),
            pltpu.SemaphoreType.DMA((3 + 2 * exp_count,)),
            pltpu.SemaphoreType.DMA((5 + parts,)),
        ],
        name="own_sums",
    )(kernel_index, strip_bounds, basis_bank, exposures, inv_variance)

    received = lax.all_to_all(sums, "epoch", 0, 0, tiled=True, axis_index_groups=groups)

    from_core = lax.ppermute(to_core, "patch", [(at, at ^ 1) for at in range(patches)])
    from_link = lax.ppermute(to_link, "patch", [(at, ((at + 1) ^ 1) - 1) for at in range(1, patches - 1)])
    keep_shape, give_shape = shape(near, 2 * EDGE, share, dtype=f32), shape(near, 2 * EDGE, share)
    vmem_spec = pl.BlockSpec(memory_space=pltpu.VMEM)
    strip_keep, strip_give = pl.pallas_call(
        strip_sums,
        out_shape=(keep_shape, give_shape),
        in_specs=[vmem_spec, vmem_spec, hbm, hbm, hbm, hbm],
        out_specs=(vmem_spec,) * 2,
        scratch_shapes=[
            *[vmem(strip)] * 2,
            vmem(edge_rows),
            vmem(row_mat),
            vmem(edge_mat),
            pltpu.VMEM((exp_count, 2 * EDGE, width + LANES), bf16),
            pltpu.VMEM((exp_count, 2 * NCOMP * EDGE, width), bf16),
            pltpu.SemaphoreType.DMA((5,)),
        ],
        compiler_params=pltpu.CompilerParams(vmem_limit_bytes=12 * 1024 * 1024),
        name="strip_sums",
    )(from_core, from_link, inv_variance, strips, row_mats, edge_mats)
    received, strip_give = lax.optimization_barrier((received, strip_give))
    received = received.reshape(near, FAR, lines, share)

    def half(at):
        return jnp.sum(lax.dynamic_index_in_dim(received, at, 1, keepdims=False).astype(f32), axis=0)

    keep, give = half(far), half(1 - far).astype(bf16)
    inner = keep + lax.ppermute(give, "epoch", swap).astype(f32)
    strip_sum = (strip_keep + lax.ppermute(strip_give, "epoch", swap).astype(f32)).astype(bf16)

    strip_parts = lax.all_to_all(strip_sum, "epoch", 0, 0, tiled=True, axis_index_groups=groups)
    edges = jnp.sum(strip_parts.astype(f32), axis=0)

    numer = jnp.concatenate([edges[:EDGE], inner[:INNER], edges[EDGE:]], axis=0)
    denom = inner[INNER:]
    return numer / jnp.maximum(denom, 1.0), denom


def solution(mesh):
    return jax.shard_map(
        shards,
        mesh=mesh,
        in_specs=(
            P(("band", "epoch"), "patch", None),
            P(("band", "epoch"), "patch", None),
            P(("band", "epoch"), None),
            P(("band", "epoch"), None, None),
            P(),
        ),
        out_specs=(P(("band", "patch"), "epoch"), P(("band", "patch"), "epoch")),
        check_vma=False,
    )
```
